32 devices in a mesh: dp: 4 (over x, core), wide: 8 (over z, y).
Axes of the slice: x: 2, y: 2, z: 4, core: 2. Of those that a mesh axis runs over, the one named last changes fastest.
Arguments:
- tokens: bfloat16 [32768, 16384], P('dp', 'wide'), may hold values from -6 to 6
- cotangent: bfloat16 [32768, 16384], P('dp', 'wide'), may hold values from -6 to 6
- left_factor: bfloat16 [128, 128, 128], P('wide', 'dp'), may hold values from -0.5 to 0.5
- right_factor: bfloat16 [128, 128, 128], P('wide', 'dp'), may hold values from -0.5 to 0.5
- column_map: int32 [16384], replicated, may hold values from 0 to 16383, as said below
Outputs:
- grad_tokens: bfloat16 [32768, 16384], P('dp', 'wide')
- grad_left: float32 [128, 128, 128], P('wide', 'dp')
- grad_right: float32 [128, 128, 128], P('wide', 'dp')
The draws below stay inside these ranges and needn't reach their ends.
Inputs may be any that keep to these rules, and one draw needn't show every extreme that they name: column_map[c * 128 + r] = block_order[r] * 128 + lane_order[c] for two permutations block_order and lane_order of 0 to 127: column r of output block c takes lane lane_order[c] of input block block_order[r].
All inputs are finite; a program needn't handle non-finite values.
Results may differ from the reference program's by a relative error of at most 0.0057.
Values may be sent and summed in bfloat16 or wider, within the bound.
No kernel may reach another device: no remote copies, remote signals or barrier semaphores. Data moves between devices by JAX's collectives and lax.ppermute only.
A program may use at most 256 MiB of HBM per device.

```python
import jax
import jax.numpy as jnp
from jax import lax

BLK = 128
D = 16384
NBLK = 128
TOKENS = 32768


def draw_column_map(key, part):
    key = jax.random.fold_in(key, 7)
    first_key, second_key = jax.random.split(key)
    lane_order = jax.random.permutation(first_key, BLK)
    block_order = jax.random.permutation(second_key, BLK)
    table = block_order[None, :] * BLK + lane_order[:, None]
    return table.reshape(-1).astype(jnp.int32)


def steps_of(rng, shape, cuts, smallest, top_value):
    def one(axis_at, parts):
        draws = jax.random.uniform(jax.random.fold_in(jax.random.fold_in(rng, 6), axis_at), (parts,), jnp.float32, smallest / len(cuts), top_value / len(cuts))
        return jnp.repeat(jnp.exp(draws), shape[axis_at] // parts).reshape((-1,) + (1,) * (len(shape) - axis_at - 1))

    factor_of = one(*cuts[0])
    for cut in cuts[1:]:
        factor_of = factor_of * one(*cut)
    return factor_of


def noise(own_key, shape, width, reach, shards=(), held_as=jnp.bfloat16):
    entries = jax.random.normal(own_key, shape, jnp.float32) * width
    if len(shards) > 0:
        entries = steps_of(own_key, shape, shards, -0.22, 0.18) * entries
    return jnp.clip(entries, min=-reach, max=reach).astype(held_as)


def setup_inputs(seed: int = 0) -> dict:
    key_list = jax.random.split(jax.random.key(seed), 6)
    tokens = noise(key_list[0], (TOKENS, D), 1.0, 6.0, ((0, 4), (1, 8)))
    cotangent = noise(key_list[1], (TOKENS, D), 1.0, 6.0, ((0, 4), (1, 8)))
    left_factor = noise(key_list[2], (NBLK, BLK, BLK), BLK ** -0.5, 0.5, ((0, 8), (1, 4)))
    right_factor = noise(key_list[3], (NBLK, BLK, BLK), BLK ** -0.5, 0.5, ((0, 8), (1, 4)))
    column_map = draw_column_map(jax.random.fold_in(key_list[5], 71), 0)
    return dict(tokens=tokens, cotangent=cotangent, left_factor=left_factor, right_factor=right_factor, column_map=column_map)


gelu_scale = 0.7978845608
gelu_cubic = 0.044715


def gelu_parts(value):
    tanh_part = jnp.tanh(gelu_scale * (value + gelu_cubic * value * value * value))
    result = 0.5 * value * (1.0 + tanh_part)
    slope = 0.5 * (1.0 + tanh_part) + 0.5 * value * (1.0 - tanh_part * tanh_part) * gelu_scale * (1.0 + 3.0 * gelu_cubic * value * value)
    return result, slope


def reference(tokens, cotangent, left_factor, right_factor, column_map):
    token_count = tokens.shape[0]
    block_rows = min(token_count, 2048)
    block_count = token_count // block_rows
    inverse_map = jnp.zeros((D,), jnp.int32).at[column_map].set(jnp.arange(D, dtype=jnp.int32))
    left_wide = left_factor.astype(jnp.float32)
    right_wide = right_factor.astype(jnp.float32)

    def advance(totals, pair):
        left_total, right_total = totals
        x_rows, g_rows = pair
        x_blocks = x_rows.astype(jnp.float32).reshape(block_rows, NBLK, BLK)
        pre_act = jnp.einsum('tbi,bij->tbj', x_blocks, left_wide)
        activated, slope = gelu_parts(pre_act)
        hidden = activated.astype(jnp.bfloat16).reshape(block_rows, D)
        mixed = hidden[:, column_map].reshape(block_rows, NBLK, BLK).astype(jnp.float32)
        g_blocks = g_rows.astype(jnp.float32).reshape(block_rows, NBLK, BLK)
        right_total = right_total + jnp.einsum('tci,tcj->cij', mixed, g_blocks)
        d_mixed = jnp.einsum('tcj,cij->tci', g_blocks, right_wide).astype(jnp.bfloat16).reshape(block_rows, D)
        d_hidden = d_mixed[:, inverse_map].reshape(block_rows, NBLK, BLK).astype(jnp.float32)
        d_pre_low = (d_hidden * slope).astype(jnp.bfloat16)
        d_pre = lax.optimization_barrier(d_pre_low).astype(jnp.float32)
        left_total = left_total + jnp.einsum('tbi,tbj->bij', x_blocks, d_pre)
        grad_rows = jnp.einsum('tbj,bij->tbi', d_pre, left_wide).astype(jnp.bfloat16).reshape(block_rows, D)
        return (left_total, right_total), grad_rows

    start = (jnp.zeros((NBLK, BLK, BLK), jnp.float32), jnp.zeros((NBLK, BLK, BLK), jnp.float32))
    totals, grad_blocks = lax.scan(advance, start, (tokens.reshape(block_count, block_rows, D), cotangent.reshape(block_count, block_rows, D)))
    return grad_blocks.reshape(token_count, D), totals[0], totals[1]
```

```python
import functools

import jax
import jax.numpy as jnp
from jax import lax
from jax.experimental import pallas as pl
from jax.experimental.pallas import tpu as pltpu
from jax.sharding import PartitionSpec as P

gelu_scale = 0.7978845608
gelu_cubic = 0.044715
f32 = jnp.float32
bf16 = jnp.bfloat16
lane_count = 128


def gelu_tanh(value):
    return jnp.tanh(gelu_scale * (value + gelu_cubic * value * value * value))


def gelu_value(value):
    return 0.5 * value * (1.0 + gelu_tanh(value))


def gelu_slope(value):
    tanh_part = gelu_tanh(value)
    return 0.5 * (1.0 + tanh_part) + 0.5 * value * (1.0 - tanh_part * tanh_part) * gelu_scale * (
        1.0 + 3.0 * gelu_cubic * value * value
    )


def dot(a, b, a_dim, b_dim, precision=None):
    return lax.dot_general(
        a, b, (((a_dim,), (b_dim,)), ((), ())), precision=precision, preferred_element_type=f32
    )


def params(steps):
    return pltpu.CompilerParams(
        dimension_semantics=("arbitrary",) * steps, vmem_limit_bytes=48 * 1024 * 1024
    )


def cost(flops, bytes_accessed, transcendentals=0):
    return pl.CostEstimate(
        flops=int(flops), bytes_accessed=int(bytes_accessed), transcendentals=int(transcendentals)
    )


def after(value, earlier):
    return value if earlier is None else lax.optimization_barrier((value, earlier))[0]


def exchange(send):
    return lax.all_to_all(send, "wide", split_axis=0, concat_axis=0, tiled=True)


def cuts(total, weights, unit=1):
    edges, done = [0], 0
    for weight in weights:
        done += weight
        edges.append(total * done // sum(weights) // unit * unit)
    return [(a, b) for a, b in zip(edges[:-1], edges[1:]) if b > a]


def right_sent_kernel(map_ref, factor_ref, out_ref):
    size = factor_ref.shape[1]
    order = map_ref[0:1, :] // size
    pick = jnp.where(lax.broadcasted_iota(jnp.int32, (size, size), 0) == order, 1.0, 0.0).astype(bf16)
    for c in range(factor_ref.shape[0]):
        out_ref[c] = dot(pick, factor_ref[c], 1, 0).astype(bf16)


def left_sent_kernel(map_ref, factor_ref, out_ref):
    size = factor_ref.shape[1]
    order = map_ref[:, 0:1] % size
    pick = jnp.where(lax.broadcasted_iota(jnp.int32, (size, size), 1) == order, 1.0, 0.0).astype(bf16)
    for b in range(factor_ref.shape[0]):
        out_ref[b] = dot(pick, factor_ref[b], 1, 1).astype(bf16)


def left_done_kernel(map_ref, total_ref, *refs):
    out_refs, rows_ref = refs[:-1], refs[-1]
    size = total_ref.shape[1]
    order = map_ref[:, 0:1] % size
    pick = jnp.where(lax.broadcasted_iota(jnp.int32, (size, size), 1) == order, 1.0, 0.0)
    for b in range(total_ref.shape[0]):
        rows_ref[...] = dot(total_ref[b], pick, 0, 0, lax.Precision.HIGHEST)
        share_out(rows_ref, out_refs, b)


def share_out(rows_ref, out_refs, at):
    rows = rows_ref.shape[0] // len(out_refs)
    own = lax.axis_index("dp")
    for s, out_ref in enumerate(out_refs):
        out_ref[at] = rows_ref[pl.ds(pl.multiple_of((own ^ s) * rows, rows), rows), :]


def left_done(grid_map, total):
    dp = lax.axis_size("dp")
    blocks, size, _ = total.shape
    return pl.pallas_call(
        left_done_kernel,
        out_shape=[jax.ShapeDtypeStruct((blocks, size // dp, size), f32)] * dp,
        scratch_shapes=[pltpu.VMEM((size, size), f32)],
        cost_estimate=cost(12 * total.size * size, 8 * total.size),
        compiler_params=params(0),
    )(grid_map, total)


def ordered(kernel, grid_map, factor):
    return pl.pallas_call(
        kernel,
        out_shape=jax.ShapeDtypeStruct(factor.shape, bf16),
        cost_estimate=cost(2 * factor.size * factor.shape[2], 4 * factor.size),
        compiler_params=params(0),
    )(grid_map, factor)


def send_kernel(activate, x_ref, w_ref, out_ref, wide_ref):
    blocks, size = w_ref.shape[0], w_ref.shape[-1]
    dests, count = w_ref.shape[1], w_ref.shape[2]
    width = dests * count
    pieces = wide_ref.shape[0]
    pitch = wide_ref.shape[1] // blocks
    for p in range(blocks):
        factor = w_ref[p].reshape(width, size)
        y = dot(factor, x_ref[:, p * size : (p + 1) * size], 1, 1)
        if activate:
            y = gelu_value(y)
        for k in range(pieces):
            wide_ref[k, p * pitch : p * pitch + width, :] = y[:, k * lane_count : (k + 1) * lane_count]
    for dest in range(dests):
        for n in range(count):
            for k in range(pieces):
                rows = wide_ref[k, pl.ds(dest * count + n, blocks, stride=pitch), :]
                out_ref[dest, n, :, k * lane_count : (k + 1) * lane_count] = rows.astype(bf16)


def send_part(x, factor, rows, part, activate, tile):
    blocks, wide, _, size = factor.shape
    (start, stop), (first, last) = rows, part
    count, length = last - first, stop - start
    width = wide * count
    taken = factor[:, :, first:last]
    pitch = -(-width // 8) * 8 + 8
    return pl.pallas_call(
        functools.partial(send_kernel, activate),
        grid=(length // tile,),
        in_specs=[
            pl.BlockSpec((tile, blocks * size), lambda i: (start // tile + i, 0)),
            pl.BlockSpec((blocks, wide, count, size), lambda i: (0, 0, 0, 0)),
        ],
        out_specs=pl.BlockSpec((wide, count, blocks, tile), lambda i: (0, 0, 0, i)),
        out_shape=jax.ShapeDtypeStruct((wide, count, blocks, length), bf16),
        scratch_shapes=[pltpu.VMEM((tile // lane_count, blocks * pitch, lane_count), f32)],
        cost_estimate=cost(
            2 * length * blocks * width * size,
            2 * length * blocks * (size + width),
            length * blocks * width if activate else 0,
        ),
        compiler_params=params(1),
    )(x, taken)


def right_kernel(map_ref, received_ref, g_ref, *refs):
    out_refs, rows_ref = refs[:-1], refs[-1]
    size = g_ref.shape[1]
    total = dot(received_ref[:, 0].reshape(size, received_ref.shape[3]), g_ref[...], 1, 0)
    order = map_ref[0:1, :] // size
    pick = jnp.where(lax.broadcasted_iota(jnp.int32, (size, size), 0) == order, 1.0, 0.0)
    rows_ref[...] = dot(pick, total, 0, 0, lax.Precision.HIGHEST)
    share_out(rows_ref, out_refs, 0)


def right_part(grid_map, received, cotangent, part, first):
    dp = lax.axis_size("dp")
    wide, _, blocks, length = received.shape
    size = grid_map.shape[0]
    count, skip = part[1] - part[0], part[0] - first
    return pl.pallas_call(
        right_kernel,
        grid=(count,),
        in_specs=[
            pl.BlockSpec((size, size), lambda n: (0, 0)),
            pl.BlockSpec((wide, 1, blocks, length), lambda n: (0, skip + n, 0, 0)),
            pl.BlockSpec((length, size), lambda n: (0, part[0] + n)),
        ],
        out_specs=[pl.BlockSpec((1, size // dp, size), lambda n: (n, 0, 0))] * dp,
        out_shape=[jax.ShapeDtypeStruct((count, size // dp, size), f32)] * dp,
        scratch_shapes=[pltpu.VMEM((size, size), f32)],
        cost_estimate=cost(2 * count * size * size * length, 4 * count * size * length),
        compiler_params=params(1),
    )(grid_map, received, cotangent)


def back_kernel(has_total, received_ref, x_ref, w_ref, *refs):
    if has_total:
        _, earlier_ref, rows_ref, total_ref = refs
    else:
        rows_ref, total_ref = refs
    blocks, size = w_ref.shape[0], w_ref.shape[1]
    tile = x_ref.shape[0]

    @pl.when(pl.program_id(0) == 0)
    def _():
        if has_total:
            total_ref[...] = earlier_ref[...]
        else:
            total_ref[...] = jnp.zeros_like(total_ref)

    for b in range(blocks):
        x = x_ref[:, b * size : (b + 1) * size]
        slope = gelu_slope(dot(w_ref[b], x, 1, 1))
        d_hidden = received_ref[:, b].reshape(size, tile).astype(f32)
        d_pre = (d_hidden * slope).astype(bf16)
        total_ref[b] += dot(d_pre, x, 1, 0)
        rows_ref[:, b * size : (b + 1) * size] = dot(d_pre, w_ref[b], 0, 0).astype(bf16)


def back_part(received, tokens, factor, rows, earlier, tile):
    wide, blocks, _, length = received.shape
    size = factor.shape[1]
    start = rows[0] // tile
    whole_factor = pl.BlockSpec((blocks, size, size), lambda i: (0, 0, 0))
    in_specs = [
        pl.BlockSpec((wide, blocks, blocks, tile), lambda i: (0, 0, 0, i)),
        pl.BlockSpec((tile, blocks * size), lambda i: (start + i, 0)),
        whole_factor,
    ]
    operands = [received, tokens, factor]
    aliases = {}
    if earlier is not None:
        in_specs += [pl.BlockSpec(memory_space=pl.ANY), whole_factor]
        operands += list(earlier)
        aliases = {3: 0}
    return pl.pallas_call(
        functools.partial(back_kernel, earlier is not None),
        grid=(length // tile,),
        in_specs=in_specs,
        out_specs=[pl.BlockSpec((tile, blocks * size), lambda i: (start + i, 0)), whole_factor],
        out_shape=[
            jax.ShapeDtypeStruct(tokens.shape, bf16),
            jax.ShapeDtypeStruct((blocks, size, size), f32),
        ],
        input_output_aliases=aliases,
        cost_estimate=cost(
            6 * length * blocks * size * size, 6 * length * blocks * size, length * blocks * size
        ),
        compiler_params=params(1),
    )(*operands)


def sum_over_dp(pieces):
    total = pieces[0]
    for s in range(1, len(pieces)):
        total = total + lax.ppermute(pieces[s], "dp", [(i, i ^ s) for i in range(len(pieces))])
    return total


def with_kernels(tokens, cotangent, left_factor, right_factor, column_map):
    row_count = tokens.shape[0]
    blocks = left_factor.shape[0]
    size = left_factor.shape[2]
    wide = lax.axis_size("wide")
    tile = 512

    grid_map = column_map.reshape(size, size)
    right_full = lax.all_gather(right_factor, "dp", axis=1, tiled=True)
    right_sent = ordered(right_sent_kernel, grid_map, right_full)
    left_full = lax.all_gather(left_factor, "dp", axis=1, tiled=True)
    left_sent = ordered(left_sent_kernel, grid_map, left_full)
    by_dest = (blocks, wide, blocks, size)
    everything = (0, row_count)

    row_cuts = cuts(row_count, row_weights, tile)
    block_cuts = cuts(blocks, block_weights)
    last, arrived = None, []
    for rows in row_cuts:
        send = send_part(cotangent, right_sent.reshape(by_dest), rows, (0, blocks), False, tile)
        last = exchange(after(send, last))
        arrived.append(last)

    received = []
    for part in block_cuts[:-1]:
        send = send_part(tokens, left_sent.reshape(by_dest), everything, part, True, tile)
        last = exchange(after(send, last))
        received.append(last)

    earlier = None
    for rows, got in zip(row_cuts, arrived):
        earlier = back_part(got, tokens, left_sent, rows, earlier, tile)
    grad_tokens, left_total = earlier
    left_share = sum_over_dp(left_done(grid_map, left_total))

    part = block_cuts[-1]
    send = send_part(tokens, left_sent.reshape(by_dest), everything, part, True, tile)
    last = exchange(after(send, (last, left_share)))

    shares = []
    for (first, stop), got in zip(block_cuts, received):
        half = (first + stop) // 2
        for piece in ((first, half), (half, stop)):
            if piece[1] > piece[0]:
                shares.append(sum_over_dp(right_part(grid_map, got, cotangent, piece, first)))
    shares.append(sum_over_dp(right_part(grid_map, last, cotangent, part, part[0])))
    return (grad_tokens, left_share, jnp.concatenate(shares, axis=0))


row_weights = (1, 15)
block_weights = (15, 1)


def plain(tokens, cotangent, left_factor, right_factor, column_map):
    row_count = tokens.shape[0]
    blocks = left_factor.shape[0]
    size = left_factor.shape[2]
    wide = lax.axis_size("wide")

    grid = column_map.reshape(size, size)
    block_order = grid[0] // size
    lane_order = grid[:, 0] % size
    counting = jnp.arange(size, dtype=jnp.int32)
    lane_pick = (lane_order[:, None] == counting[None, :]).astype(bf16)
    block_pick = (block_order[None, :] == counting[:, None]).astype(bf16)
    lane_inverse = jnp.sum(jnp.where(lane_order[None, :] == counting[:, None], counting[None, :], 0), axis=1)

    right_full = lax.all_gather(right_factor, "dp", axis=1, tiled=True)
    left_full = lax.all_gather(left_factor, "dp", axis=1, tiled=True)
    left_sent = jnp.einsum("cl,bil->bci", lane_pick, left_full, preferred_element_type=f32).astype(bf16)
    right_sent = jnp.einsum("br,crj->cbj", block_pick, right_full, preferred_element_type=f32).astype(bf16)

    x_blocks = tokens.reshape(row_count, blocks, size)
    g_blocks = cotangent.reshape(row_count, blocks, size)

    d_mixed = jnp.einsum("tcj,cbj->cbt", g_blocks, right_sent, preferred_element_type=f32)
    d_mixed = d_mixed.astype(bf16).reshape(blocks, wide, blocks, row_count)
    arrived = exchange(d_mixed.transpose(1, 2, 0, 3))

    pre_act = jnp.einsum("tbi,bci->bct", x_blocks, left_sent, preferred_element_type=f32)
    hidden = gelu_value(pre_act).astype(bf16).reshape(blocks, wide, blocks, row_count)
    received = exchange(after(hidden.transpose(1, 2, 0, 3), arrived))

    d_hidden = arrived.transpose(1, 0, 2, 3).reshape(blocks, size, row_count)
    d_pre = (d_hidden.astype(f32) * gelu_slope(pre_act)).astype(bf16)
    left_total = jnp.einsum("bct,tbi->bic", d_pre, x_blocks, preferred_element_type=f32)
    grad_tokens = jnp.einsum("bct,bci->tbi", d_pre, left_sent, preferred_element_type=f32)
    left_share = lax.psum_scatter(left_total, "dp", scatter_dimension=1, tiled=True)
    left_share = jnp.take(left_share, lane_inverse, axis=2)

    right_total = jnp.einsum("snbt,tnj->nsbj", received, g_blocks, preferred_element_type=f32)
    right_total = jnp.take(right_total.reshape(blocks, size, size), block_order, axis=1)
    right_share = lax.psum_scatter(right_total, "dp", scatter_dimension=1, tiled=True)
    return (grad_tokens.astype(bf16).reshape(row_count, blocks * size), left_share, right_share)


def shards(*args):
    blocks, size = args[2].shape[0], args[2].shape[2]
    dp = lax.axis_size("dp")
    fits = blocks % 16 == 0 and size == lane_count and dp & (dp - 1) == 0 and size % (8 * dp) == 0
    return (with_kernels if fits else plain)(*args)


def solution(mesh):
    return jax.shard_map(
        shards,
        mesh=mesh,
        in_specs=(
            P("dp", "wide"),
            P("dp", "wide"),
            P("wide", "dp", None),
            P("wide", "dp", None),
            P(),
        ),
        out_specs=(P("dp", "wide"), P("wide", "dp", None), P("wide", "dp", None)),
        check_vma=False,
    )
```

```python
import functools

import jax
import jax.numpy as jnp
from jax import lax
from jax.experimental import pallas as pl
from jax.experimental.pallas import tpu as pltpu
from jax.sharding import PartitionSpec as P

gelu_scale = 0.7978845608
gelu_cubic = 0.044715
f32 = jnp.float32
bf16 = jnp.bfloat16
lane_count = 128


def gelu_tanh(value):
    return jnp.tanh(gelu_scale * (value + gelu_cubic * value * value * value))


def gelu_value(value):
    return 0.5 * value * (1.0 + gelu_tanh(value))


def gelu_slope(value):
    tanh_part = gelu_tanh(value)
    return 0.5 * (1.0 + tanh_part) + 0.5 * value * (1.0 - tanh_part * tanh_part) * gelu_scale * (
        1.0 + 3.0 * gelu_cubic * value * value
    )


def dot(a, b, a_dim, b_dim, precision=None):
    return lax.dot_general(
        a, b, (((a_dim,), (b_dim,)), ((), ())), precision=precision, preferred_element_type=f32
    )


def params(steps):
    return pltpu.CompilerParams(
        dimension_semantics=("arbitrary",) * steps, vmem_limit_bytes=48 * 1024 * 1024
    )


def cost(flops, bytes_accessed, transcendentals=0):
    return pl.CostEstimate(
        flops=int(flops), bytes_accessed=int(bytes_accessed), transcendentals=int(transcendentals)
    )


def after(value, earlier):
    return value if earlier is None else lax.optimization_barrier((value, earlier))[0]


def exchange(send):
    return lax.all_to_all(send, "wide", split_axis=0, concat_axis=0, tiled=True)


def cuts(total, weights, unit=1):
    edges, done = [0], 0
    for weight in weights:
        done += weight
        edges.append(total * done // sum(weights) // unit * unit)
    return [(a, b) for a, b in zip(edges[:-1], edges[1:]) if b > a]


def right_sent_kernel(map_ref, factor_ref, out_ref):
    size = factor_ref.shape[1]
    order = map_ref[0:1, :] // size
    pick = jnp.where(lax.broadcasted_iota(jnp.int32, (size, size), 0) == order, 1.0, 0.0).astype(bf16)
    for c in range(factor_ref.shape[0]):
        out_ref[c] = dot(pick, factor_ref[c], 1, 0).astype(bf16)


def left_sent_kernel(map_ref, factor_ref, out_ref):
    size = factor_ref.shape[1]
    order = map_ref[:, 0:1] % size
    pick = jnp.where(lax.broadcasted_iota(jnp.int32, (size, size), 1) == order, 1.0, 0.0).astype(bf16)
    for b in range(factor_ref.shape[0]):
        out_ref[b] = dot(pick, factor_ref[b], 1, 1).astype(bf16)


def left_done_kernel(map_ref, total_ref, *refs):
    out_refs, rows_ref = refs[:-1], refs[-1]
    size = total_ref.shape[1]
    order = map_ref[:, 0:1] % size
    pick = jnp.where(lax.broadcasted_iota(jnp.int32, (size, size), 1) == order, 1.0, 0.0)
    for b in range(total_ref.shape[0]):
        rows_ref[...] = dot(total_ref[b], pick, 0, 0, lax.Precision.HIGHEST)
        share_out(rows_ref, out_refs, b)


def share_out(rows_ref, out_refs, at):
    rows = rows_ref.shape[0] // len(out_refs)
    own = lax.axis_index("dp")
    for s, out_ref in enumerate(out_refs):
        out_ref[at] = rows_ref[pl.ds(pl.multiple_of((own ^ s) * rows, rows), rows), :]


def left_done(grid_map, total):
    dp = lax.axis_size("dp")
    blocks, size, _ = total.shape
    return pl.pallas_call(
        left_done_kernel,
        out_shape=[jax.ShapeDtypeStruct((blocks, size // dp, size), f32)] * dp,
        scratch_shapes=[pltpu.VMEM((size, size), f32)],
        cost_estimate=cost(12 * total.size * size, 8 * total.size),
        compiler_params=params(0),
    )(grid_map, total)


def ordered(kernel, grid_map, factor):
    return pl.pallas_call(
        kernel,
        out_shape=jax.ShapeDtypeStruct(factor.shape, bf16),
        cost_estimate=cost(2 * factor.size * factor.shape[2], 4 * factor.size),
        compiler_params=params(0),
    )(grid_map, factor)


def send_kernel(activate, x_ref, w_ref, *refs):
    out_refs, wide_ref = refs[:-1], refs[-1]
    blocks, size = w_ref.shape[0], w_ref.shape[-1]
    dests, count = w_ref.shape[1], w_ref.shape[2]
    width = dests * count
    pieces = wide_ref.shape[0]
    pitch = wide_ref.shape[1] // blocks
    for p in range(blocks):
        factor = w_ref[p].reshape(width, size)
        y = dot(factor, x_ref[:, p * size : (p + 1) * size], 1, 1)
        if activate:
            y = gelu_value(y)
        for k in range(pieces):
            wide_ref[k, p * pitch : p * pitch + width, :] = y[:, k * lane_count : (k + 1) * lane_count]
    for dest in range(dests):
        for n in range(count):
            for k in range(pieces):
                rows = wide_ref[k, pl.ds(dest * count + n, blocks, stride=pitch), :]
                out = out_refs[0].at[dest] if len(out_refs) == 1 else out_refs[dest]
                out[n, :, k * lane_count : (k + 1) * lane_count] = rows.astype(bf16)


def send_part(x, factor, rows, part, activate, tile, apart=False):
    blocks, wide, _, size = factor.shape
    (start, stop), (first, last) = rows, part
    count, length = last - first, stop - start
    width = wide * count
    taken = factor[:, :, first:last]
    if apart:
        taken = jnp.take(taken, lax.axis_index("wide") ^ jnp.arange(wide, dtype=jnp.int32), axis=1)
        out_specs = [pl.BlockSpec((count, blocks, tile), lambda i: (0, 0, i))] * wide
        out_shape = [jax.ShapeDtypeStruct((count, blocks, length), bf16)] * wide
    else:
        out_specs = pl.BlockSpec((wide, count, blocks, tile), lambda i: (0, 0, 0, i))
        out_shape = jax.ShapeDtypeStruct((wide, count, blocks, length), bf16)
    pitch = -(-width // 8) * 8 + 8
    return pl.pallas_call(
        functools.partial(send_kernel, activate),
        grid=(length // tile,),
        in_specs=[
            pl.BlockSpec((tile, blocks * size), lambda i: (start // tile + i, 0)),
            pl.BlockSpec((blocks, wide, count, size), lambda i: (0, 0, 0, 0)),
        ],
        out_specs=out_specs,
        out_shape=out_shape,
        scratch_shapes=[pltpu.VMEM((tile // lane_count, blocks * pitch, lane_count), f32)],
        cost_estimate=cost(
            2 * length * blocks * width * size,
            2 * length * blocks * (size + width),
            length * blocks * width if activate else 0,
        ),
        compiler_params=params(1),
    )(x, taken)


def right_kernel(apart, map_ref, *refs):
    count = apart or 1
    received_refs, g_ref, out_refs, rows_ref = refs[:count], refs[count], refs[count + 1 : -1], refs[-1]
    size, length = g_ref.shape[1], g_ref.shape[0]
    block = lax.broadcasted_iota(jnp.int32, (size, size), 0)
    if apart:
        rows = jnp.concatenate([ref[0] for ref in received_refs], axis=0)
        block = block ^ (lax.axis_index("wide") * received_refs[0].shape[1])
    else:
        rows = received_refs[0][:, 0].reshape(size, length)
    total = dot(rows, g_ref[...], 1, 0)
    pick = jnp.where(block == map_ref[0:1, :] // size, 1.0, 0.0)
    rows_ref[...] = dot(pick, total, 0, 0, lax.Precision.HIGHEST)
    share_out(rows_ref, out_refs, 0)


def right_part(grid_map, received, cotangent, part, first):
    dp = lax.axis_size("dp")
    size = grid_map.shape[0]
    length = cotangent.shape[0]
    count, skip = part[1] - part[0], part[0] - first
    if isinstance(received, list):
        apart = len(received)
        blocks = received[0].shape[1]
        specs = [pl.BlockSpec((1, blocks, length), lambda n: (skip + n, 0, 0))] * apart
    else:
        apart = 0
        wide, _, blocks, _ = received.shape
        specs = [pl.BlockSpec((wide, 1, blocks, length), lambda n: (0, skip + n, 0, 0))]
        received = [received]
    out_specs = [pl.BlockSpec((1, size // dp, size), lambda n: (n, 0, 0))] * dp
    out_shape = [jax.ShapeDtypeStruct((count, size // dp, size), f32)] * dp
    return pl.pallas_call(
        functools.partial(right_kernel, apart),
        grid=(count,),
        in_specs=[
            pl.BlockSpec((size, size), lambda n: (0, 0)),
            *specs,
            pl.BlockSpec((length, size), lambda n: (0, part[0] + n)),
        ],
        out_specs=out_specs,
        out_shape=out_shape,
        scratch_shapes=[pltpu.VMEM((size, size), f32)],
        cost_estimate=cost(2 * count * size * size * length, 4 * count * size * length),
        compiler_params=params(1),
    )(grid_map, *received, cotangent)


def back_kernel(apart, has_total, *refs):
    count = apart or 1
    received_refs, x_ref, w_ref = refs[:count], refs[count], refs[count + 1]
    refs = refs[count + 2 :]
    if apart:
        *refs, turned_ref = refs
    if has_total:
        _, earlier_ref, rows_ref, total_ref = refs
    else:
        rows_ref, total_ref = refs
    blocks, size = w_ref.shape[0], w_ref.shape[1]
    tile = x_ref.shape[0]

    @pl.when(pl.program_id(0) == 0)
    def _():
        if has_total:
            total_ref[...] = earlier_ref[...]
        else:
            total_ref[...] = jnp.zeros_like(total_ref)

    for b in range(blocks):
        x = x_ref[:, b * size : (b + 1) * size]
        slope = gelu_slope(dot(w_ref[b], x, 1, 1))
        if apart:
            for s, ref in enumerate(received_refs):
                first = (lax.axis_index("wide") ^ s) * blocks
                turned_ref[pl.ds(pl.multiple_of(first, blocks), blocks), :] = ref[b]
            d_hidden = turned_ref[...].astype(f32)
        else:
            d_hidden = received_refs[0][:, b].reshape(size, tile).astype(f32)
        d_pre = (d_hidden * slope).astype(bf16)
        total_ref[b] += dot(d_pre, x, 1, 0)
        rows_ref[:, b * size : (b + 1) * size] = dot(d_pre, w_ref[b], 0, 0).astype(bf16)


def back_part(received, tokens, factor, rows, earlier, tile):
    blocks, size, _ = factor.shape
    length = rows[1] - rows[0]
    start = rows[0] // tile
    whole_factor = pl.BlockSpec((blocks, size, size), lambda i: (0, 0, 0))
    scratch = []
    if isinstance(received, list):
        apart = len(received)
        specs = [pl.BlockSpec((blocks, blocks, tile), lambda i: (0, 0, i))] * apart
        scratch = [pltpu.VMEM((size, tile), bf16)]
    else:
        apart = 0
        specs = [pl.BlockSpec((received.shape[0], blocks, blocks, tile), lambda i: (0, 0, 0, i))]
        received = [received]
    in_specs = specs + [
        pl.BlockSpec((tile, blocks * size), lambda i: (start + i, 0)),
        whole_factor,
    ]
    operands = [*received, tokens, factor]
    aliases = {}
    if earlier is not None:
        in_specs += [pl.BlockSpec(memory_space=pl.ANY), whole_factor]
        operands += list(earlier)
        aliases = {len(received) + 2: 0}
    return pl.pallas_call(
        functools.partial(back_kernel, apart, earlier is not None),
        grid=(length // tile,),
        in_specs=in_specs,
        out_specs=[pl.BlockSpec((tile, blocks * size), lambda i: (start + i, 0)), whole_factor],
        out_shape=[
            jax.ShapeDtypeStruct(tokens.shape, bf16),
            jax.ShapeDtypeStruct((blocks, size, size), f32),
        ],
        scratch_shapes=scratch,
        input_output_aliases=aliases,
        cost_estimate=cost(
            back_hint * 6 * length * blocks * size * size, 6 * length * blocks * size, length * blocks * size
        ),
        compiler_params=params(1),
    )(*operands)


def sum_over_dp(pieces):
    total = pieces[0]
    for s in range(1, len(pieces)):
        total = total + lax.ppermute(pieces[s], "dp", [(i, i ^ s) for i in range(len(pieces))])
    return total


def with_kernels(tokens, cotangent, left_factor, right_factor, column_map):
    row_count = tokens.shape[0]
    blocks = left_factor.shape[0]
    size = left_factor.shape[2]
    wide = lax.axis_size("wide")
    tile = 512

    by_dest = (blocks, wide, blocks, size)
    everything = (0, row_count)
    far, near = range(wide // 2, wide), range(1, wide // 2)
    head, body = cuts(row_count, row_weights, tile)
    main, filler, final = cuts(blocks, block_weights)

    def move(piece, s):
        return lax.ppermute(piece, "wide", [(i, i ^ s) for i in range(wide)])

    grid_map = column_map.reshape(size, size)
    right_full = lax.all_gather(right_factor, "dp", axis=1, tiled=True)
    right_sent = ordered(right_sent_kernel, grid_map, right_full).reshape(by_dest)
    send = send_part(cotangent, right_sent, head, (0, blocks), False, tile)
    got_head = exchange(send)
    right_sent = after(right_sent, send)
    got_body = exchange(after(send_part(cotangent, right_sent, body, (0, blocks), False, tile), got_head))

    left_full = lax.all_gather(left_factor, "dp", axis=1, tiled=True)
    left_sent = ordered(left_sent_kernel, grid_map, left_full)
    left_by_dest = left_sent.reshape(by_dest)
    apart = send_part(tokens, left_by_dest, everything, filler, True, tile, True)
    got_filler = {0: apart[0], **{s: move(apart[s], s) for s in far}}
    rest = send_part(tokens, after(left_by_dest, apart[0]), everything, main, True, tile)
    got_main = exchange(after(rest, got_body))

    arrived = tuple(got_filler[s] for s in far)
    left_then = after(left_sent, arrived)
    earlier = back_part(got_head, tokens, left_then, head, None, tile)
    got_filler |= {s: move(after(apart[s], earlier[1]), s) for s in near}
    grad_tokens, left_total = back_part(got_body, tokens, left_sent, body, earlier, tile)
    arrived = tuple(got_filler[s] for s in near)
    left_share = sum_over_dp(left_done(after(grid_map, arrived), left_total))
    send = send_part(tokens, left_by_dest, everything, final, True, tile)
    got_final = exchange(after(send, (got_main, left_share)))

    def share(part, got, begin):
        return sum_over_dp(right_part(grid_map, got, cotangent, part, begin))

    middle = (main[0] + main[1]) // 2
    shares = [
        share((main[0], middle), got_main, main[0]),
        share((middle, main[1]), got_main, main[0]),
        share(filler, [got_filler[s] for s in range(wide)], filler[0]),
        share(final, got_final, final[0]),
    ]
    return (grad_tokens, left_share, jnp.concatenate(shares, axis=0))


back_hint = 41.75
row_weights = (1, 15)
block_weights = (14, 1, 1)


def plain(tokens, cotangent, left_factor, right_factor, column_map):
    row_count = tokens.shape[0]
    blocks = left_factor.shape[0]
    size = left_factor.shape[2]
    wide = lax.axis_size("wide")

    grid = column_map.reshape(size, size)
    block_order = grid[0] // size
    lane_order = grid[:, 0] % size
    counting = jnp.arange(size, dtype=jnp.int32)
    lane_pick = (lane_order[:, None] == counting[None, :]).astype(bf16)
    block_pick = (block_order[None, :] == counting[:, None]).astype(bf16)
    lane_inverse = jnp.sum(jnp.where(lane_order[None, :] == counting[:, None], counting[None, :], 0), axis=1)

    right_full = lax.all_gather(right_factor, "dp", axis=1, tiled=True)
    left_full = lax.all_gather(left_factor, "dp", axis=1, tiled=True)
    left_sent = jnp.einsum("cl,bil->bci", lane_pick, left_full, preferred_element_type=f32).astype(bf16)
    right_sent = jnp.einsum("br,crj->cbj", block_pick, right_full, preferred_element_type=f32).astype(bf16)

    x_blocks = tokens.reshape(row_count, blocks, size)
    g_blocks = cotangent.reshape(row_count, blocks, size)

    d_mixed = jnp.einsum("tcj,cbj->cbt", g_blocks, right_sent, preferred_element_type=f32)
    d_mixed = d_mixed.astype(bf16).reshape(blocks, wide, blocks, row_count)
    arrived = exchange(d_mixed.transpose(1, 2, 0, 3))

    pre_act = jnp.einsum("tbi,bci->bct", x_blocks, left_sent, preferred_element_type=f32)
    hidden = gelu_value(pre_act).astype(bf16).reshape(blocks, wide, blocks, row_count)
    received = exchange(after(hidden.transpose(1, 2, 0, 3), arrived))

    d_hidden = arrived.transpose(1, 0, 2, 3).reshape(blocks, size, row_count)
    d_pre = (d_hidden.astype(f32) * gelu_slope(pre_act)).astype(bf16)
    left_total = jnp.einsum("bct,tbi->bic", d_pre, x_blocks, preferred_element_type=f32)
    grad_tokens = jnp.einsum("bct,bci->tbi", d_pre, left_sent, preferred_element_type=f32)
    left_share = lax.psum_scatter(left_total, "dp", scatter_dimension=1, tiled=True)
    left_share = jnp.take(left_share, lane_inverse, axis=2)

    right_total = jnp.einsum("snbt,tnj->nsbj", received, g_blocks, preferred_element_type=f32)
    right_total = jnp.take(right_total.reshape(blocks, size, size), block_order, axis=1)
    right_share = lax.psum_scatter(right_total, "dp", scatter_dimension=1, tiled=True)
    return (grad_tokens.astype(bf16).reshape(row_count, blocks * size), left_share, right_share)


def shards(*args):
    blocks, size = args[2].shape[0], args[2].shape[2]
    dp = lax.axis_size("dp")
    wide = lax.axis_size("wide")
    powers = dp & (dp - 1) == 0 and wide & (wide - 1) == 0 and wide > 1
    fits = blocks % 16 == 0 and blocks & (blocks - 1) == 0 and size == lane_count and size % (8 * dp) == 0
    return (with_kernels if fits and powers else plain)(*args)


def solution(mesh):
    return jax.shard_map(
        shards,
        mesh=mesh,
        in_specs=(
            P("dp", "wide"),
            P("dp", "wide"),
            P("wide", "dp", None),
            P("wide", "dp", None),
            P(),
        ),
        out_specs=(P("dp", "wide"), P("wide", "dp", None), P("wide", "dp", None)),
        check_vma=False,
    )
```

```python
import functools

import jax
import jax.numpy as jnp
from jax import lax
from jax.experimental import pallas as pl
from jax.experimental.pallas import tpu as pltpu
from jax.sharding import PartitionSpec as P

gelu_scale = 0.7978845608
gelu_cubic = 0.044715
f32 = jnp.float32
bf16 = jnp.bfloat16
lane_count = 128


def gelu_tanh(value):
    return jnp.tanh(gelu_scale * (value + gelu_cubic * value * value * value))


def gelu_value(value):
    return 0.5 * value * (1.0 + gelu_tanh(value))


def gelu_slope(value):
    tanh_part = gelu_tanh(value)
    return 0.5 * (1.0 + tanh_part) + 0.5 * value * (1.0 - tanh_part * tanh_part) * gelu_scale * (
        1.0 + 3.0 * gelu_cubic * value * value
    )


def dot(a, b, a_dim, b_dim, precision=None):
    return lax.dot_general(
        a, b, (((a_dim,), (b_dim,)), ((), ())), precision=precision, preferred_element_type=f32
    )


def params(steps):
    return pltpu.CompilerParams(
        dimension_semantics=("arbitrary",) * steps, vmem_limit_bytes=48 * 1024 * 1024
    )


def cost(flops, bytes_accessed, transcendentals=0):
    return pl.CostEstimate(
        flops=int(flops), bytes_accessed=int(bytes_accessed), transcendentals=int(transcendentals)
    )


def after(value, earlier):
    return value if earlier is None else lax.optimization_barrier((value, earlier))[0]


def exchange(send):
    return lax.all_to_all(send, "wide", split_axis=0, concat_axis=0, tiled=True)


def cuts(total, weights, unit=1):
    edges, done = [0], 0
    for weight in weights:
        done += weight
        edges.append(total * done // sum(weights) // unit * unit)
    return [(a, b) for a, b in zip(edges[:-1], edges[1:]) if b > a]


def right_sent_kernel(map_ref, factor_ref, out_ref):
    size = factor_ref.shape[1]
    order = map_ref[0:1, :] // size
    pick = jnp.where(lax.broadcasted_iota(jnp.int32, (size, size), 0) == order, 1.0, 0.0).astype(bf16)
    for c in range(factor_ref.shape[0]):
        out_ref[c] = dot(pick, factor_ref[c], 1, 0).astype(bf16)


def left_sent_kernel(map_ref, factor_ref, out_ref):
    size = factor_ref.shape[1]
    order = map_ref[:, 0:1] % size
    pick = jnp.where(lax.broadcasted_iota(jnp.int32, (size, size), 1) == order, 1.0, 0.0).astype(bf16)
    for b in range(factor_ref.shape[0]):
        out_ref[b] = dot(pick, factor_ref[b], 1, 1).astype(bf16)


def left_done_kernel(map_ref, total_ref, *refs):
    out_refs, rows_ref = refs[:-1], refs[-1]
    size = total_ref.shape[1]
    order = map_ref[:, 0:1] % size
    pick = jnp.where(lax.broadcasted_iota(jnp.int32, (size, size), 1) == order, 1.0, 0.0)
    for b in range(total_ref.shape[0]):
        rows_ref[...] = dot(total_ref[b], pick, 0, 0, lax.Precision.HIGHEST)
        share_out(rows_ref, out_refs, b)


def share_out(rows_ref, out_refs, at):
    rows = rows_ref.shape[0] // len(out_refs)
    own = lax.axis_index("dp")
    for s, out_ref in enumerate(out_refs):
        out_ref[at] = rows_ref[pl.ds(pl.multiple_of((own ^ s) * rows, rows), rows), :]


def left_done(grid_map, total):
    dp = lax.axis_size("dp")
    blocks, size, _ = total.shape
    return pl.pallas_call(
        left_done_kernel,
        out_shape=[jax.ShapeDtypeStruct((blocks, size // dp, size), f32)] * dp,
        scratch_shapes=[pltpu.VMEM((size, size), f32)],
        cost_estimate=cost(12 * total.size * size, 8 * total.size),
        compiler_params=params(0),
    )(grid_map, total)


def ordered(kernel, grid_map, factor):
    return pl.pallas_call(
        kernel,
        out_shape=jax.ShapeDtypeStruct(factor.shape, bf16),
        cost_estimate=cost(2 * factor.size * factor.shape[2], 4 * factor.size),
        compiler_params=params(0),
    )(grid_map, factor)


def send_kernel(activate, x_ref, w_ref, *refs):
    out_refs, wide_ref = refs[:-1], refs[-1]
    blocks, size = w_ref.shape[0], w_ref.shape[-1]
    dests, count = w_ref.shape[1], w_ref.shape[2]
    width = dests * count
    pieces = wide_ref.shape[0]
    pitch = wide_ref.shape[1] // blocks
    for p in range(blocks):
        factor = w_ref[p].reshape(width, size)
        y = dot(factor, x_ref[:, p * size : (p + 1) * size], 1, 1)
        if activate:
            y = gelu_value(y)
        for k in range(pieces):
            wide_ref[k, p * pitch : p * pitch + width, :] = y[:, k * lane_count : (k + 1) * lane_count]
    for dest in range(dests):
        for n in range(count):
            for k in range(pieces):
                rows = wide_ref[k, pl.ds(dest * count + n, blocks, stride=pitch), :]
                out = out_refs[0].at[dest] if len(out_refs) == 1 else out_refs[dest]
                out[n, :, k * lane_count : (k + 1) * lane_count] = rows.astype(bf16)


def send_part(x, factor, rows, part, activate, tile, apart=False):
    blocks, wide, _, size = factor.shape
    (start, stop), (first, last) = rows, part
    count, length = last - first, stop - start
    width = wide * count
    taken = factor[:, :, first:last]
    if apart:
        taken = jnp.take(taken, lax.axis_index("wide") ^ jnp.arange(wide, dtype=jnp.int32), axis=1)
        out_specs = [pl.BlockSpec((count, blocks, tile), lambda i: (0, 0, i))] * wide
        out_shape = [jax.ShapeDtypeStruct((count, blocks, length), bf16)] * wide
    else:
        out_specs = pl.BlockSpec((wide, count, blocks, tile), lambda i: (0, 0, 0, i))
        out_shape = jax.ShapeDtypeStruct((wide, count, blocks, length), bf16)
    pitch = -(-width // 8) * 8 + 8
    return pl.pallas_call(
        functools.partial(send_kernel, activate),
        grid=(length // tile,),
        in_specs=[
            pl.BlockSpec((tile, blocks * size), lambda i: (start // tile + i, 0)),
            pl.BlockSpec((blocks, wide, count, size), lambda i: (0, 0, 0, 0)),
        ],
        out_specs=out_specs,
        out_shape=out_shape,
        scratch_shapes=[pltpu.VMEM((tile // lane_count, blocks * pitch, lane_count), f32)],
        cost_estimate=cost(
            (send_hint if activate and count > 1 else 1) * 2 * length * blocks * width * size,
            2 * length * blocks * (size + width),
            length * blocks * width if activate else 0,
        ),
        compiler_params=params(1),
    )(x, taken)


def right_kernel(apart, map_ref, *refs):
    count = apart or 1
    received_refs, g_ref, out_refs, rows_ref = refs[:count], refs[count], refs[count + 1 : -1], refs[-1]
    size, length = g_ref.shape[1], g_ref.shape[0]
    block = lax.broadcasted_iota(jnp.int32, (size, size), 0)
    if apart:
        rows = jnp.concatenate([ref[0] for ref in received_refs], axis=0)
        block = block ^ (lax.axis_index("wide") * received_refs[0].shape[1])
    else:
        rows = received_refs[0][:, 0].reshape(size, length)
    total = dot(rows, g_ref[...], 1, 0)
    pick = jnp.where(block == map_ref[0:1, :] // size, 1.0, 0.0)
    rows_ref[...] = dot(pick, total, 0, 0, lax.Precision.HIGHEST)
    share_out(rows_ref, out_refs, 0)


def right_part(grid_map, received, cotangent, part, first):
    dp = lax.axis_size("dp")
    size = grid_map.shape[0]
    length = cotangent.shape[0]
    count, skip = part[1] - part[0], part[0] - first
    if isinstance(received, list):
        apart = len(received)
        blocks = received[0].shape[1]
        specs = [pl.BlockSpec((1, blocks, length), lambda n: (skip + n, 0, 0))] * apart
    else:
        apart = 0
        wide, _, blocks, _ = received.shape
        specs = [pl.BlockSpec((wide, 1, blocks, length), lambda n: (0, skip + n, 0, 0))]
        received = [received]
    out_specs = [pl.BlockSpec((1, size // dp, size), lambda n: (n, 0, 0))] * dp
    out_shape = [jax.ShapeDtypeStruct((count, size // dp, size), f32)] * dp
    return pl.pallas_call(
        functools.partial(right_kernel, apart),
        grid=(count,),
        in_specs=[
            pl.BlockSpec((size, size), lambda n: (0, 0)),
            *specs,
            pl.BlockSpec((length, size), lambda n: (0, part[0] + n)),
        ],
        out_specs=out_specs,
        out_shape=out_shape,
        scratch_shapes=[pltpu.VMEM((size, size), f32)],
        cost_estimate=cost(2 * count * size * size * length, 4 * count * size * length),
        compiler_params=params(1),
    )(grid_map, *received, cotangent)


def back_kernel(apart, has_total, *refs):
    count = apart or 1
    received_refs, x_ref, w_ref = refs[:count], refs[count], refs[count + 1]
    refs = refs[count + 2 :]
    if apart:
        *refs, turned_ref = refs
    if has_total:
        _, earlier_ref, rows_ref, total_ref = refs
    else:
        rows_ref, total_ref = refs
    blocks, size = w_ref.shape[0], w_ref.shape[1]
    tile = x_ref.shape[0]

    @pl.when(pl.program_id(0) == 0)
    def _():
        if has_total:
            total_ref[...] = earlier_ref[...]
        else:
            total_ref[...] = jnp.zeros_like(total_ref)

    for b in range(blocks):
        x = x_ref[:, b * size : (b + 1) * size]
        slope = gelu_slope(dot(w_ref[b], x, 1, 1))
        if apart:
            for s, ref in enumerate(received_refs):
                first = (lax.axis_index("wide") ^ s) * blocks
                turned_ref[pl.ds(pl.multiple_of(first, blocks), blocks), :] = ref[b]
            d_hidden = turned_ref[...].astype(f32)
        else:
            d_hidden = received_refs[0][:, b].reshape(size, tile).astype(f32)
        d_pre = (d_hidden * slope).astype(bf16)
        total_ref[b] += dot(d_pre, x, 1, 0)
        rows_ref[:, b * size : (b + 1) * size] = dot(d_pre, w_ref[b], 0, 0).astype(bf16)


def back_part(received, tokens, factor, rows, earlier, tile):
    blocks, size, _ = factor.shape
    length = rows[1] - rows[0]
    start = rows[0] // tile
    whole_factor = pl.BlockSpec((blocks, size, size), lambda i: (0, 0, 0))
    scratch = []
    if isinstance(received, list):
        apart = len(received)
        specs = [pl.BlockSpec((blocks, blocks, tile), lambda i: (0, 0, i))] * apart
        scratch = [pltpu.VMEM((size, tile), bf16)]
    else:
        apart = 0
        specs = [pl.BlockSpec((received.shape[0], blocks, blocks, tile), lambda i: (0, 0, 0, i))]
        received = [received]
    in_specs = specs + [
        pl.BlockSpec((tile, blocks * size), lambda i: (start + i, 0)),
        whole_factor,
    ]
    operands = [*received, tokens, factor]
    aliases = {}
    if earlier is not None:
        in_specs += [pl.BlockSpec(memory_space=pl.ANY), whole_factor]
        operands += list(earlier)
        aliases = {len(received) + 2: 0}
    return pl.pallas_call(
        functools.partial(back_kernel, apart, earlier is not None),
        grid=(length // tile,),
        in_specs=in_specs,
        out_specs=[pl.BlockSpec((tile, blocks * size), lambda i: (start + i, 0)), whole_factor],
        out_shape=[
            jax.ShapeDtypeStruct(tokens.shape, bf16),
            jax.ShapeDtypeStruct((blocks, size, size), f32),
        ],
        scratch_shapes=scratch,
        input_output_aliases=aliases,
        cost_estimate=cost(
            back_hint * 6 * length * blocks * size * size, 6 * length * blocks * size, length * blocks * size
        ),
        compiler_params=params(1),
    )(*operands)


def sum_over_dp(pieces):
    total = pieces[0]
    for s in range(1, len(pieces)):
        total = total + lax.ppermute(pieces[s], "dp", [(i, i ^ s) for i in range(len(pieces))])
    return total


def with_kernels(tokens, cotangent, left_factor, right_factor, column_map):
    row_count = tokens.shape[0]
    blocks = left_factor.shape[0]
    size = left_factor.shape[2]
    wide = lax.axis_size("wide")
    tile = 512

    by_dest = (blocks, wide, blocks, size)
    everything = (0, row_count)
    far, near = range(wide // 2, wide), range(1, wide // 2)
    head, body = cuts(row_count, row_weights, tile)
    main, filler, final = cuts(blocks, block_weights)

    def move(piece, s):
        return lax.ppermute(piece, "wide", [(i, i ^ s) for i in range(wide)])

    grid_map = column_map.reshape(size, size)
    right_full = lax.all_gather(right_factor, "dp", axis=1, tiled=True)
    right_sent = ordered(right_sent_kernel, grid_map, right_full).reshape(by_dest)
    mixed = send_part(cotangent, right_sent, head, (0, blocks), False, tile, True)
    got_head = {0: mixed[0], **{s: move(mixed[s], s) for s in far}}
    right_sent = after(right_sent, mixed[0])
    got_body = exchange(send_part(cotangent, right_sent, body, (0, blocks), False, tile))

    arrived = tuple(got_head[s] for s in far)
    left_full = lax.all_gather(after(left_factor, arrived), "dp", axis=1, tiled=True)
    got_head |= {s: move(after(mixed[s], arrived), s) for s in near}
    left_sent = ordered(left_sent_kernel, grid_map, left_full)
    left_by_dest = left_sent.reshape(by_dest)
    left_by_dest = after(left_by_dest, tuple(got_head[s] for s in near))
    apart = send_part(tokens, left_by_dest, everything, filler, True, tile, True)
    got_filler = {0: apart[0], **{s: move(apart[s], s) for s in far}}
    rest = send_part(tokens, after(left_by_dest, apart[0]), everything, main, True, tile)
    got_main = exchange(after(rest, got_body))

    arrived = tuple(got_filler[s] for s in far)
    left_then = after(left_sent, arrived)
    earlier = back_part([got_head[s] for s in range(wide)], tokens, left_then, head, None, tile)
    got_filler |= {s: move(after(apart[s], earlier[1]), s) for s in near}
    grad_tokens, left_total = back_part(got_body, tokens, left_sent, body, earlier, tile)
    arrived = tuple(got_filler[s] for s in near)
    left_share = sum_over_dp(left_done(after(grid_map, arrived), left_total))
    send = send_part(tokens, left_by_dest, everything, final, True, tile)
    got_final = exchange(after(send, (got_main, left_share)))

    def share(part, got, begin):
        return sum_over_dp(right_part(grid_map, got, cotangent, part, begin))

    middle = (main[0] + main[1]) // 2
    shares = [
        share((main[0], middle), got_main, main[0]),
        share((middle, main[1]), got_main, main[0]),
        share(filler, [got_filler[s] for s in range(wide)], filler[0]),
        share(final, got_final, final[0]),
    ]
    return (grad_tokens, left_share, jnp.concatenate(shares, axis=0))


back_hint = 41.75
send_hint = 154.062
row_weights = (1, 15)
block_weights = (14, 1, 1)


def plain(tokens, cotangent, left_factor, right_factor, column_map):
    row_count = tokens.shape[0]
    blocks = left_factor.shape[0]
    size = left_factor.shape[2]
    wide = lax.axis_size("wide")

    grid = column_map.reshape(size, size)
    block_order = grid[0] // size
    lane_order = grid[:, 0] % size
    counting = jnp.arange(size, dtype=jnp.int32)
    lane_pick = (lane_order[:, None] == counting[None, :]).astype(bf16)
    block_pick = (block_order[None, :] == counting[:, None]).astype(bf16)
    lane_inverse = jnp.sum(jnp.where(lane_order[None, :] == counting[:, None], counting[None, :], 0), axis=1)

    right_full = lax.all_gather(right_factor, "dp", axis=1, tiled=True)
    left_full = lax.all_gather(left_factor, "dp", axis=1, tiled=True)
    left_sent = jnp.einsum("cl,bil->bci", lane_pick, left_full, preferred_element_type=f32).astype(bf16)
    right_sent = jnp.einsum("br,crj->cbj", block_pick, right_full, preferred_element_type=f32).astype(bf16)

    x_blocks = tokens.reshape(row_count, blocks, size)
    g_blocks = cotangent.reshape(row_count, blocks, size)

    d_mixed = jnp.einsum("tcj,cbj->cbt", g_blocks, right_sent, preferred_element_type=f32)
    d_mixed = d_mixed.astype(bf16).reshape(blocks, wide, blocks, row_count)
    arrived = exchange(d_mixed.transpose(1, 2, 0, 3))

    pre_act = jnp.einsum("tbi,bci->bct", x_blocks, left_sent, preferred_element_type=f32)
    hidden = gelu_value(pre_act).astype(bf16).reshape(blocks, wide, blocks, row_count)
    received = exchange(after(hidden.transpose(1, 2, 0, 3), arrived))

    d_hidden = arrived.transpose(1, 0, 2, 3).reshape(blocks, size, row_count)
    d_pre = (d_hidden.astype(f32) * gelu_slope(pre_act)).astype(bf16)
    left_total = jnp.einsum("bct,tbi->bic", d_pre, x_blocks, preferred_element_type=f32)
    grad_tokens = jnp.einsum("bct,bci->tbi", d_pre, left_sent, preferred_element_type=f32)
    left_share = lax.psum_scatter(left_total, "dp", scatter_dimension=1, tiled=True)
    left_share = jnp.take(left_share, lane_inverse, axis=2)

    right_total = jnp.einsum("snbt,tnj->nsbj", received, g_blocks, preferred_element_type=f32)
    right_total = jnp.take(right_total.reshape(blocks, size, size), block_order, axis=1)
    right_share = lax.psum_scatter(right_total, "dp", scatter_dimension=1, tiled=True)
    return (grad_tokens.astype(bf16).reshape(row_count, blocks * size), left_share, right_share)


def shards(*args):
    blocks, size = args[2].shape[0], args[2].shape[2]
    dp = lax.axis_size("dp")
    wide = lax.axis_size("wide")
    powers = dp & (dp - 1) == 0 and wide & (wide - 1) == 0 and wide > 1
    fits = blocks % 16 == 0 and blocks & (blocks - 1) == 0 and size == lane_count and size % (8 * dp) == 0
    return (with_kernels if fits and powers else plain)(*args)


def solution(mesh):
    return jax.shard_map(
        shards,
        mesh=mesh,
        in_specs=(
            P("dp", "wide"),
            P("dp", "wide"),
            P("wide", "dp", None),
            P("wide", "dp", None),
            P(),
        ),
        out_specs=(P("dp", "wide"), P("wide", "dp", None), P("wide", "dp", None)),
        check_vma=False,
    )
```
